32 devices in a mesh: grp: 4 (over z), loc: 4 (over y, core), tp: 2 (over x).
Axes of the slice: x: 2, y: 2, z: 4, core: 2. Of those that a mesh axis runs over, the one named last changes fastest.
Arguments:
- tokens: bfloat16 [2048, 2048], P(('grp', 'tp')), may hold values from -6 to 6
- expert_ids: int32 [2048, 8], P(('grp', 'tp')), may hold values from 0 to 15, as said below
- router_weights: bfloat16 [2048, 8], P(('grp', 'tp')), may hold values from 0.19921875 to 1
- w_gate: bfloat16 [16, 2048, 768], P(('grp', 'loc')), may hold values from -0.125 to 0.125
- w_up: bfloat16 [16, 2048, 768], P(('grp', 'loc')), may hold values from -0.125 to 0.125
- w_down: bfloat16 [16, 768, 2048], P(('grp', 'loc'), None, 'tp'), may hold values from -0.21875 to 0.21875
Outputs:
- mixed: bfloat16 [2048, 2048], P(('grp', 'tp'), 'loc')
The draws below stay inside these ranges and needn't reach their ends.
Inputs may be any that keep to these rules, and one draw needn't show every extreme that they name: `expert_ids`: each row names 8 different experts, two from each of 4 different groups, group g holding experts g * 4 to g * 4 + 3. Within each aligned block of 256 rows, no expert is named by more than 128 rows, and in every block some expert is named by exactly 128 rows.
All inputs are finite; a program needn't handle non-finite values.
Results may differ from the reference program's by a relative error of at most 0.0057.
Values may be sent and summed in bfloat16 or wider, within the bound.
No kernel may reach another device: no remote copies, remote signals or barrier semaphores. Data moves between devices by JAX's collectives and lax.ppermute only.
A program may use at most 64 MiB of HBM per device.

```python
import math
import jax
import jax.numpy as jnp
from jax import lax

D = 2048
FF = 768
TOPK = 8
TOPG = 4
TOK_DEV = 256
TOKENS = 2048
GROUPS = 4
GROUP_SIZE = 4
EXPERTS = 16
CAP = 128


def block_routes(key):
    quantum = TOK_DEV // GROUPS
    top_lift = quantum * min(2, GROUPS - 4)
    pair_count = GROUPS // 2
    key_lift, key_label, key_extra, key_shuffle = jax.random.split(key, 4)
    lifted = jax.random.randint(key_lift, (pair_count,), 0, top_lift + 1).astype(jnp.int32)
    lifted = lifted.at[0].set(top_lift)
    group_counts = jnp.concatenate([4 * quantum + lifted, (4 * quantum - lifted)[::-1]]).astype(jnp.int32)
    group_ends = jnp.cumsum(group_counts).astype(jnp.int32)
    group_starts = group_ends - group_counts
    position = jnp.arange(TOPG * TOK_DEV, dtype=jnp.int32)
    run_index = jnp.sum((position[:, None] >= group_ends[None, :]).astype(jnp.int32), axis=1).astype(jnp.int32)
    within_run = position - group_starts[run_index]
    run_size = group_counts[run_index]
    base_load = 2 * group_counts // GROUP_SIZE
    extra_load = 2 * group_counts % GROUP_SIZE
    extra_rank = jax.vmap(lambda sub_key: jax.random.permutation(sub_key, GROUP_SIZE))(jax.random.split(key_extra, GROUPS)).astype(jnp.int32)
    expert_loads = base_load[:, None] + (extra_rank < extra_load[:, None]).astype(jnp.int32)
    run_ends = jnp.cumsum(expert_loads, axis=1).astype(jnp.int32)
    chosen_ends = run_ends[run_index]
    first_local = jnp.sum((within_run[:, None] >= chosen_ends).astype(jnp.int32), axis=1).astype(jnp.int32)
    second_local = jnp.sum(((within_run + run_size)[:, None] >= chosen_ends).astype(jnp.int32), axis=1).astype(jnp.int32)
    group_label = jax.random.permutation(key_label, GROUPS).astype(jnp.int32)
    group_id = group_label[run_index]
    pair_ids = jnp.stack([group_id * GROUP_SIZE + first_local, group_id * GROUP_SIZE + second_local], axis=-1)
    pair_ids = pair_ids.reshape(TOPG, TOK_DEV, 2).transpose(1, 0, 2).reshape(TOK_DEV, TOPK)
    shuffle = jax.random.permutation(key_shuffle, TOK_DEV)
    return pair_ids[shuffle].astype(jnp.int32)


def draw_expert_ids(key, part):
    block_count = TOKENS // TOK_DEV
    block_keys = jax.random.split(key, block_count)
    routed = jax.vmap(block_routes)(block_keys)
    return routed.reshape(TOKENS, TOPK).astype(jnp.int32)


def shard_levels(own_key, extent, shards, low, top_value):
    factor_of = 1.0
    for dim, shards_of in shards:
        heights = jax.random.uniform(jax.random.fold_in(jax.random.fold_in(own_key, 6), dim), (shards_of,), jnp.float32, low / len(shards), top_value / len(shards))
        factor_of = factor_of * jnp.repeat(jnp.exp(heights), extent[dim] // shards_of).reshape((-1,) + (1,) * (len(extent) - 1 - dim))
    return factor_of


def normal_values(own_key, shape, deviation, limit, cuts=(), kind=jnp.bfloat16):
    array = jax.random.normal(own_key, shape, jnp.float32) * deviation
    if len(cuts) > 0:
        array = shard_levels(own_key, shape, cuts, -0.22, 0.18) * array
    return jnp.clip(array, min=-limit, max=limit).astype(kind)


def setup_inputs(seed: int = 0) -> dict:
    seeds = jax.random.split(jax.random.key(seed), 7)
    tokens = normal_values(seeds[0], (TOKENS, D), 1.0, 6.0, ((0, 8),))
    expert_ids = draw_expert_ids(jax.random.fold_in(seeds[6], 71), 0)
    router_weights = jnp.clip(jnp.exp(math.log(1.0) - 1.6133518 * jax.random.uniform(seeds[2], (TOKENS, TOPK), jnp.float32) ** shard_levels(seeds[2], (TOKENS, TOPK), ((0, 8),), -0.2, 0.2)), 0.19921875, 1.0).astype(jnp.bfloat16)
    w_gate = normal_values(seeds[3], (EXPERTS, D, FF), D ** -0.5, 0.125, ((0, 16),))
    w_up = normal_values(seeds[4], (EXPERTS, D, FF), D ** -0.5, 0.125, ((0, 16),))
    w_down = normal_values(seeds[5], (EXPERTS, FF, D), FF ** -0.5, 0.21875, ((0, 16), (2, 2)))
    return {"tokens": tokens, "expert_ids": expert_ids, "router_weights": router_weights, "w_gate": w_gate, "w_up": w_up, "w_down": w_down}


def reference(tokens, expert_ids, router_weights, w_gate, w_up, w_down):
    block_count = TOKENS // TOK_DEV
    entry_total = TOKENS * TOPK
    expert_block = expert_ids.reshape(block_count, TOK_DEV * TOPK)
    hit_table = (expert_block[:, :, None] == jnp.arange(EXPERTS, dtype=jnp.int32)[None, None, :]).astype(jnp.int32)
    slot_rank = (jnp.sum(jnp.cumsum(hit_table, axis=1) * hit_table, axis=2) - 1).astype(jnp.int32)
    slot_index = (jnp.arange(block_count, dtype=jnp.int32)[:, None] * CAP + slot_rank).reshape(-1).astype(jnp.int32)
    token_row = (jnp.arange(entry_total, dtype=jnp.int32) // TOPK).astype(jnp.int32)
    flat_expert = expert_ids.reshape(-1).astype(jnp.int32)
    slot_width = block_count * CAP
    row_table = jnp.full((EXPERTS, slot_width), TOKENS, jnp.int32).at[flat_expert, slot_index].set(token_row)
    scale_table = jnp.zeros((EXPERTS, slot_width), jnp.float32).at[flat_expert, slot_index].set(
        router_weights.reshape(-1).astype(jnp.float32))
    padded = jnp.concatenate([tokens, jnp.zeros((1, D), tokens.dtype)], axis=0)

    def one_expert(running, expert_inputs):
        row_ids, gate_scale, gate_matrix, up_matrix, down_matrix = expert_inputs
        chosen = padded[row_ids]
        gate_act = jnp.dot(chosen, gate_matrix, preferred_element_type=jnp.float32)
        upward = jnp.dot(chosen, up_matrix, preferred_element_type=jnp.float32)
        hidden = (jax.nn.silu(gate_act) * upward).astype(jnp.bfloat16)
        expert_out = jnp.dot(hidden, down_matrix, preferred_element_type=jnp.float32)
        rounded = lax.optimization_barrier(expert_out.astype(jnp.bfloat16)).astype(jnp.float32)
        running = running.at[row_ids].add(gate_scale[:, None] * rounded)
        return running, None

    start_sum = jnp.zeros((TOKENS + 1, D), jnp.float32)
    running, _ = lax.scan(one_expert, start_sum, (row_table, scale_table, w_gate, w_up, w_down))
    return running[:TOKENS].astype(jnp.bfloat16)
```

```python
import jax
import jax.numpy as jnp
from jax import lax
from jax.sharding import PartitionSpec as P


def swap_bit(value, axis, bit):
    size = lax.axis_size(axis)
    return lax.ppermute(value, axis, [(i, i ^ bit) for i in range(size)])


def shift_by(value, axis, step):
    size = lax.axis_size(axis)
    return lax.ppermute(value, axis, [(i, (i + step) % size) for i in range(size)])


def bits_of(size):
    return [1 << i for i in range(size.bit_length() - 1)]


def body(tokens, expert_ids, router_weights, w_gate, w_up, w_down):
    groups = lax.axis_size("grp")
    group_size = lax.axis_size("loc")
    tp_size = lax.axis_size("tp")
    own_group = lax.axis_index("grp")
    own_local = lax.axis_index("loc")
    own_tp = lax.axis_index("tp")
    rows, width = tokens.shape
    part = rows // group_size
    out_cols = width // group_size
    shifts = sorted(range(1, groups), key=lambda s: -min(s, groups - s))

    mine = lax.dynamic_slice_in_dim(tokens, own_local * part, part, 0)
    sent = {s: shift_by(mine, "grp", s) for s in shifts}

    weight_of = {}
    for s in range(groups):
        target = ((own_group + s) % groups) * group_size + own_local
        hit = expert_ids == target
        dense = jnp.sum(jnp.where(hit, router_weights.astype(jnp.float32), 0.0), axis=1)
        weight_of[s] = dense.astype(jnp.bfloat16)
    for s in shifts:
        weight_of[s] = shift_by(weight_of[s], "grp", s)

    down = w_down[0]
    for bit in bits_of(tp_size):
        other = swap_bit(down, "tp", bit)
        down = jnp.where(
            own_tp & bit > 0,
            jnp.concatenate([other, down], axis=1),
            jnp.concatenate([down, other], axis=1),
        )

    def whole_block(piece):
        got = piece[None]
        order = [own_local]
        for bit in reversed(bits_of(group_size)):
            got = jnp.concatenate([got, swap_bit(got, "loc", bit)], axis=0)
        index = [0]
        for bit in reversed(bits_of(group_size)):
            index = index + [i ^ bit for i in index]
        inverse = jnp.asarray([index.index(i) for i in range(group_size)], jnp.int32)
        take = inverse[jnp.arange(group_size, dtype=jnp.int32) ^ own_local]
        return jnp.take(got, take, axis=0).reshape(rows, width)

    def ffn(block):
        gate_act = jnp.dot(block, w_gate[0], preferred_element_type=jnp.float32)
        upward = jnp.dot(block, w_up[0], preferred_element_type=jnp.float32)
        return (jax.nn.silu(gate_act) * upward).astype(jnp.bfloat16)

    hidden = {}
    for s in shifts:
        hidden[s] = ffn(whole_block(sent[s]))
    hidden[0] = ffn(tokens)

    def group_sum(s):
        scale = weight_of[s].astype(jnp.float32)[:, None]
        pieces = []
        for k in range(group_size):
            cols = lax.dynamic_slice_in_dim(down, (own_local ^ k) * out_cols, out_cols, 1)
            result = jnp.dot(hidden[s], cols, preferred_element_type=jnp.float32)
            pieces.append(result.astype(jnp.bfloat16).astype(jnp.float32) * scale)
        held = {k: pieces[k] for k in range(group_size)}
        for bit in bits_of(group_size):
            leaving = [k for k in held if k & bit]
            arrived = swap_bit(
                jnp.stack([held[k].astype(jnp.bfloat16) for k in leaving]), "loc", bit
            )
            held = {
                k ^ bit: held[k ^ bit] + arrived[n].astype(jnp.float32)
                for n, k in enumerate(leaving)
            }
        return held[0]

    total = None
    back = []
    for s in shifts:
        back.append(shift_by(group_sum(s).astype(jnp.bfloat16), "grp", groups - s))
    total = group_sum(0)
    for value in back:
        total = total + value.astype(jnp.float32)
    return total.astype(jnp.bfloat16)


def solution(mesh):
    placed = (
        P(("grp", "tp"), None),
        P(("grp", "tp"), None),
        P(("grp", "tp"), None),
        P(("grp", "loc"), None, None),
        P(("grp", "loc"), None, None),
        P(("grp", "loc"), None, "tp"),
    )
    return jax.shard_map(
        body, mesh=mesh, in_specs=placed, out_specs=P(("grp", "tp"), "loc"), check_vma=False
    )
```

```python
import functools

import jax
import jax.numpy as jnp
from jax import lax
from jax.experimental import pallas as pl
from jax.experimental.pallas import tpu as pltpu
from jax.sharding import PartitionSpec as P

VM = pl.BlockSpec(memory_space=pltpu.VMEM)
SM = pl.BlockSpec(memory_space=pltpu.SMEM)
STEP = 256


def swap_bit(value, axis, bit):
    size = lax.axis_size(axis)
    return lax.ppermute(value, axis, [(i, i ^ bit) for i in range(size)])


def shift_by(value, axis, step):
    size = lax.axis_size(axis)
    return lax.ppermute(value, axis, [(i, (i + step) % size) for i in range(size)])


def bits_of(size):
    return [1 << i for i in range(size.bit_length() - 1)]


def part_order(size):
    order = [0]
    for bit in reversed(bits_of(size)):
        order = order + [i ^ bit for i in order]
    return order


def call(kernel, outs, scratch, scalars, *arrays):
    return pl.pallas_call(
        kernel,
        out_shape=outs,
        in_specs=[SM] + [VM] * len(arrays),
        out_specs=jax.tree.map(lambda _: VM, outs),
        scratch_shapes=scratch,
        compiler_params=pltpu.CompilerParams(vmem_limit_bytes=40 << 20),
    )(scalars, *arrays)


def rows_at(index, part):
    return pl.ds(pl.multiple_of(index * part, part), part)


def hidden_kernel(order, part, scalars, *refs):
    *pieces, gate, up, hidden, block = refs
    for n, k in enumerate(order):
        if len(pieces) == 1:
            block[n * part : (n + 1) * part, :] = pieces[0][rows_at(scalars[0] ^ k, part), :]
        else:
            block[n * part : (n + 1) * part, :] = pieces[n][...]
    for j in range(0, gate.shape[1], STEP):
        a = jnp.dot(block[...], gate[:, j : j + STEP], preferred_element_type=jnp.float32)
        b = jnp.dot(block[...], up[:, j : j + STEP], preferred_element_type=jnp.float32)
        hidden[:, j : j + STEP] = (a / (1.0 + jnp.exp(-a)) * b).astype(jnp.bfloat16)


def scaled(hidden, weights, scale, j):
    out = jnp.dot(hidden[...], weights[:, j : j + STEP], preferred_element_type=jnp.float32)
    return out.astype(jnp.bfloat16).astype(jnp.float32) * scale


def scale_rows(scalars, scale, order, part):
    return jnp.concatenate([scale[rows_at(scalars[0] ^ k, part), :] for k in order], axis=0)


def leave_kernel(order, part, bit, scalars, hidden, scale, *refs):
    *columns, message = refs
    factor = scale_rows(scalars, scale, order, part)
    for u, weights in enumerate(columns):
        place = scalars[1] ^ u
        for j in range(0, weights.shape[1], STEP):
            value = scaled(hidden, weights, factor, j).astype(jnp.bfloat16)
            for n, k in enumerate(order):
                m = order.index(k ^ bit)
                message[place, n * part : (n + 1) * part, j : j + STEP] = value[m * part : (m + 1) * part]


def stay_kernel(order, part, bit, with_sum, scalars, hidden, scale, *refs):
    if with_sum:
        arrived, *refs = refs
    *columns, keep, message, total = refs
    half = len(columns) // 2
    factor = scale_rows(scalars, scale, order, part)
    for u, weights in enumerate(columns):
        place = scalars[1] ^ u
        for j in range(0, weights.shape[1], STEP):
            value = scaled(hidden, weights, factor, j)
            if with_sum:
                value = value + arrived[place, :, j : j + STEP].astype(jnp.float32)
            total[place, :, j : j + STEP] = value
    for i in range(half):
        keep[i] = total[i]
        for n, k in enumerate(order):
            m = order.index(k ^ bit)
            message[i, n * part : (n + 1) * part, :] = total[half + i, m * part : (m + 1) * part, :].astype(
                jnp.bfloat16
            )


def finish_kernel(order, part, scalars, keep, arrived, *refs):
    *others, out = refs
    for n, k in enumerate(order):
        at = slice(n * part, (n + 1) * part)
        value = keep[at, :] + arrived[at, :].astype(jnp.float32)
        for other in others:
            value = value + other[at, :].astype(jnp.float32)
        out[rows_at(scalars[0] ^ k, part), :] = value.astype(jnp.bfloat16)


def body(tokens, expert_ids, router_weights, w_gate, w_up, w_down):
    groups = lax.axis_size("grp")
    group_size = lax.axis_size("loc")
    tp_size = lax.axis_size("tp")
    own_group = lax.axis_index("grp")
    own_local = lax.axis_index("loc")
    own_tp = lax.axis_index("tp")
    rows, width = tokens.shape
    hidden_width = w_gate.shape[2]
    part = rows // group_size
    out_cols = width // group_size
    per_shard = group_size // tp_size
    order = part_order(group_size)
    shifts = sorted(range(1, groups), key=lambda s: -min(s, groups - s))
    scalars = jnp.stack([own_local, own_tp ^ (own_local // per_shard)]).astype(jnp.int32)

    down = []
    for j in reversed(range(per_shard)):
        start = ((own_local % per_shard) ^ j) * out_cols
        held = [lax.dynamic_slice_in_dim(w_down[0], start, out_cols, 1)]
        for bit in bits_of(tp_size):
            held = held + [swap_bit(value, "tp", bit) for value in held]
        down.insert(0, held)

    mine = lax.dynamic_slice_in_dim(tokens, own_local * part, part, 0)
    sent = {s: shift_by(mine, "grp", s) for s in shifts}

    scale = {}
    for s in range(groups):
        target = ((own_group + s) % groups) * group_size + own_local
        hit = expert_ids == target
        dense = jnp.sum(jnp.where(hit, router_weights.astype(jnp.float32), 0.0), axis=1)
        dense = dense.astype(jnp.bfloat16)
        if s > 0:
            dense = shift_by(dense, "grp", s)
        scale[s] = dense.astype(jnp.float32)[:, None]

    def whole_block(piece):
        pieces = [piece]
        for bit in reversed(bits_of(group_size)):
            pieces = pieces + [swap_bit(value, "loc", bit) for value in pieces]
        return pieces

    def ffn(pieces):
        return call(
            functools.partial(hidden_kernel, order, part),
            jax.ShapeDtypeStruct((rows, hidden_width), jnp.bfloat16),
            [pltpu.VMEM((rows, width), jnp.bfloat16)],
            scalars,
            *pieces,
            w_gate[0],
            w_up[0],
        )

    def group_parts(s, pieces):
        hidden = ffn(pieces)
        arrived = []
        if per_shard == 2:
            message = call(
                functools.partial(leave_kernel, order, part, 1),
                jax.ShapeDtypeStruct((tp_size, rows, out_cols), jnp.bfloat16),
                [],
                scalars,
                hidden,
                scale[s],
                *down[1],
            )
            arrived = [swap_bit(message, "loc", 1)]
        half = tp_size // 2
        keep, message = call(
            functools.partial(stay_kernel, order, part, half * per_shard, len(arrived) > 0),
            (
                jax.ShapeDtypeStruct((half, rows, out_cols), jnp.float32),
                jax.ShapeDtypeStruct((half, rows, out_cols), jnp.bfloat16),
            ),
            [pltpu.VMEM((tp_size, rows, out_cols), jnp.float32)],
            scalars,
            hidden,
            scale[s],
            *arrived,
            *down[0],
        )
        arrived = swap_bit(message, "loc", half * per_shard)
        while half > 1:
            half = half // 2
            keep = keep + arrived.astype(jnp.float32)
            bit = half * per_shard
            there = [order.index(k ^ bit) for k in order]
            message = keep[half:].astype(jnp.bfloat16).reshape(half, group_size, part, out_cols)
            message = jnp.stack([message[:, m] for m in there], axis=1)
            arrived = swap_bit(message.reshape(half, rows, out_cols), "loc", bit)
            keep = keep[:half]
        return keep[0], arrived[0]

    back = []
    for s in shifts:
        keep, arrived = group_parts(s, whole_block(sent[s]))
        both = (keep + arrived.astype(jnp.float32)).astype(jnp.bfloat16)
        back.append(shift_by(both, "grp", groups - s))
    keep, arrived = group_parts(0, [tokens])
    return call(
        functools.partial(finish_kernel, order, part),
        jax.ShapeDtypeStruct((rows, out_cols), jnp.bfloat16),
        [],
        scalars,
        keep,
        arrived,
        *back,
    )


def solution(mesh):
    placed = (
        P(("grp", "tp"), None),
        P(("grp", "tp"), None),
        P(("grp", "tp"), None),
        P(("grp", "loc"), None, None),
        P(("grp", "loc"), None, None),
        P(("grp", "loc"), None, "tp"),
    )
    return jax.shard_map(
        body, mesh=mesh, in_specs=placed, out_specs=P(("grp", "tp"), "loc"), check_vma=False
    )
```

```python
import functools

import jax
import jax.numpy as jnp
from jax import lax
from jax.experimental import pallas as pl
from jax.experimental.pallas import tpu as pltpu
from jax.sharding import PartitionSpec as P

VM = pl.BlockSpec(memory_space=pltpu.VMEM)
ANY = pl.BlockSpec(memory_space=pl.ANY)
STEP = 256
LANES = 128


def swap_bit(value, axis, bit):
    size = lax.axis_size(axis)
    return lax.ppermute(value, axis, [(i, i ^ bit) for i in range(size)])


def shift_by(value, axis, step):
    size = lax.axis_size(axis)
    return lax.ppermute(value, axis, [(i, (i + step) % size) for i in range(size)])


def bits_of(size):
    return [1 << i for i in range(size.bit_length() - 1)]


def part_order(size):
    order = [0]
    for bit in reversed(bits_of(size)):
        order = order + [i ^ bit for i in order]
    return order


def call(kernel, outs, arrays, scratch=(), in_specs=None, out_specs=None, flops=0):
    moved = sum(a.size * a.dtype.itemsize for a in (*arrays, *jax.tree.leaves(outs)))
    return pl.pallas_call(
        kernel,
        out_shape=outs,
        in_specs=in_specs or [VM] * len(arrays),
        out_specs=out_specs or jax.tree.map(lambda _: VM, outs),
        scratch_shapes=list(scratch),
        compiler_params=pltpu.CompilerParams(vmem_limit_bytes=12 << 20),
        cost_estimate=pl.CostEstimate(flops=flops, bytes_accessed=moved, transcendentals=0),
    )(*arrays)


def rows_at(index, part):
    return pl.ds(pl.multiple_of(index * part, part), part)


def own_expert():
    return lax.axis_index("grp") * lax.axis_size("loc") + lax.axis_index("loc")


def column_place(per_shard):
    return lax.axis_index("tp") ^ (lax.axis_index("loc") // per_shard)


def prepare_kernel(per_shard, part, tokens, ids, weights, down, message, table, *rest):
    *chunks, sems = rest
    width = tokens.shape[1]
    local = lax.axis_index("loc")
    copies = [
        pltpu.make_async_copy(tokens.at[rows_at(local, part), :], message.at[:, :width], sems.at[0])
    ]
    for j, chunk in enumerate(chunks):
        cols = chunk.shape[1]
        at = pl.multiple_of(((local % per_shard) ^ j) * cols, cols)
        copies.append(pltpu.make_async_copy(down.at[:, pl.ds(at, cols)], chunk, sems.at[1 + j]))
    for copy in copies:
        copy.start()
    lanes, rows = table.shape[1], table.shape[0]
    expert = lax.broadcasted_iota(jnp.int32, (lanes, rows), 0)
    dense = jnp.zeros((lanes, rows), jnp.float32)
    for k in range(ids.shape[0]):
        dense = jnp.where(expert == ids[k : k + 1, :], weights[k : k + 1, :].astype(jnp.float32), dense)
    table[...] = dense.T.astype(jnp.bfloat16)
    message[:, width:] = table[rows_at(local, part), :]
    for copy in copies:
        copy.wait()


def hidden_kernel(order, part, *refs):
    *pieces, gate, up, hidden, scale, block, routes = refs
    width = gate.shape[0]
    local = lax.axis_index("loc")
    for n, k in enumerate(order):
        at = slice(n * part, (n + 1) * part)
        if len(pieces) == 2:
            block[at, :] = pieces[0][rows_at(local ^ k, part), :]
            routes[at, :] = pieces[1][rows_at(local ^ k, part), :].astype(jnp.float32)
        else:
            block[at, :] = pieces[n][:, :width]
            routes[at, :] = pieces[n][:, width:].astype(jnp.float32)
    expert = lax.broadcasted_iota(jnp.int32, routes.shape, 1)
    own = jnp.sum(jnp.where(expert == own_expert(), routes[...], 0.0), axis=1, keepdims=True)
    scale[...] = jnp.broadcast_to(own, scale.shape)
    for j in range(0, gate.shape[1], STEP):
        a = jnp.dot(block[...], gate[:, j : j + STEP], preferred_element_type=jnp.float32)
        b = jnp.dot(block[...], up[:, j : j + STEP], preferred_element_type=jnp.float32)
        hidden[:, j : j + STEP] = (a / (1.0 + jnp.exp(-a)) * b).astype(jnp.bfloat16)


def scaled(hidden, weights, scale, j):
    out = jnp.dot(hidden[...], weights[:, j : j + STEP], preferred_element_type=jnp.float32)
    out = out.astype(jnp.bfloat16).astype(jnp.float32)
    factor = scale[...]
    return jnp.concatenate(
        [out[:, i : i + LANES] * factor for i in range(0, out.shape[1], LANES)], axis=1
    )


def leave_kernel(order, part, per_shard, bit, hidden, scale, *refs):
    *columns, message = refs
    own = column_place(per_shard)
    for u, weights in enumerate(columns):
        place = own ^ u
        for j in range(0, weights.shape[1], STEP):
            value = scaled(hidden, weights, scale, j).astype(jnp.bfloat16)
            for n, k in enumerate(order):
                m = order.index(k ^ bit)
                message[place, n * part : (n + 1) * part, j : j + STEP] = value[m * part : (m + 1) * part]


def stay_kernel(order, part, per_shard, bit, with_sum, hidden, scale, *refs):
    if with_sum:
        arrived, *refs = refs
    *columns, keep, message, total = refs
    half = len(columns) // 2
    own = column_place(per_shard)
    for u, weights in enumerate(columns):
        place = own ^ u
        for j in range(0, weights.shape[1], STEP):
            value = scaled(hidden, weights, scale, j)
            if with_sum:
                value = value + arrived[place, :, j : j + STEP].astype(jnp.float32)
            total[place, :, j : j + STEP] = value
    for i in range(half):
        keep[i] = total[i]
        for n, k in enumerate(order):
            m = order.index(k ^ bit)
            message[i, n * part : (n + 1) * part, :] = total[half + i, m * part : (m + 1) * part, :].astype(
                jnp.bfloat16
            )


def finish_kernel(order, part, keep, arrived, *refs):
    *others, out = refs
    local = lax.axis_index("loc")
    for n, k in enumerate(order):
        at = slice(n * part, (n + 1) * part)
        value = keep[at, :] + arrived[at, :].astype(jnp.float32)
        for other in others:
            value = value + other[at, :].astype(jnp.float32)
        out[rows_at(local ^ k, part), :] = value.astype(jnp.bfloat16)


def body(tokens, expert_ids, router_weights, w_gate, w_up, w_down):
    groups = lax.axis_size("grp")
    group_size = lax.axis_size("loc")
    tp_size = lax.axis_size("tp")
    rows, width = tokens.shape
    hidden_width = w_gate.shape[2]
    part = rows // group_size
    out_cols = width // group_size
    per_shard = group_size // tp_size
    lanes = -(-groups * group_size // LANES) * LANES
    order = part_order(group_size)
    shifts = sorted(range(1, groups), key=lambda s: -min(s, groups - s))
    shape = jax.ShapeDtypeStruct
    bf16, f32 = jnp.bfloat16, jnp.float32

    sliced = per_shard if per_shard > 1 else 0
    message, table, *chunks = call(
        functools.partial(prepare_kernel, per_shard, part),
        [shape((part, width + lanes), bf16), shape((rows, lanes), bf16)]
        + [shape((hidden_width, out_cols), bf16)] * sliced,
        (tokens, expert_ids.T, router_weights.T, w_down[0]),
        in_specs=[ANY, VM, VM, ANY],
        out_specs=[VM, VM] + [ANY] * sliced,
        scratch=[pltpu.SemaphoreType.DMA((1 + sliced,))],
    )
    if not chunks:
        chunks = [w_down[0]]

    down = []
    for chunk in reversed(chunks):
        held = [chunk]
        for bit in bits_of(tp_size):
            held = held + [swap_bit(value, "tp", bit) for value in held]
        down.insert(0, held)

    sent = {s: shift_by(message, "grp", s) for s in shifts}

    def whole_block(piece):
        pieces = [piece]
        for bit in reversed(bits_of(group_size)):
            pieces = pieces + [swap_bit(value, "loc", bit) for value in pieces]
        return pieces

    def ffn(pieces):
        return call(
            functools.partial(hidden_kernel, order, part),
            (shape((rows, hidden_width), bf16), shape((rows, LANES), f32)),
            (*pieces, w_gate[0], w_up[0]),
            scratch=[pltpu.VMEM((rows, width), bf16), pltpu.VMEM((rows, lanes), f32)],
            flops=4 * rows * width * hidden_width,
        )

    def group_parts(pieces):
        hidden, scale = ffn(pieces)
        flops = 2 * rows * hidden_width * out_cols * tp_size
        arrived = []
        if per_shard == 2:
            leaving = call(
                functools.partial(leave_kernel, order, part, per_shard, 1),
                shape((tp_size, rows, out_cols), bf16),
                (hidden, scale, *down[1]),
                flops=flops,
            )
            arrived = [swap_bit(leaving, "loc", 1)]
        half = tp_size // 2
        keep, leaving = call(
            functools.partial(
                stay_kernel, order, part, per_shard, half * per_shard, len(arrived) > 0
            ),
            (shape((half, rows, out_cols), f32), shape((half, rows, out_cols), bf16)),
            (hidden, scale, *arrived, *down[0]),
            scratch=[pltpu.VMEM((tp_size, rows, out_cols), f32)],
            flops=flops,
        )
        arrived = swap_bit(leaving, "loc", half * per_shard)
        while half > 1:
            half = half // 2
            keep = keep + arrived.astype(f32)
            bit = half * per_shard
            there = [order.index(k ^ bit) for k in order]
            leaving = keep[half:].astype(bf16).reshape(half, group_size, part, out_cols)
            leaving = jnp.stack([leaving[:, m] for m in there], axis=1)
            arrived = swap_bit(leaving.reshape(half, rows, out_cols), "loc", bit)
            keep = keep[:half]
        return keep[0], arrived[0]

    back = []
    for s in shifts:
        keep, arrived = group_parts(whole_block(sent[s]))
        both = (keep + arrived.astype(f32)).astype(bf16)
        back.append(shift_by(both, "grp", groups - s))
    keep, arrived = group_parts([tokens, table])
    return call(
        functools.partial(finish_kernel, order, part),
        shape((rows, out_cols), bf16),
        (keep, arrived, *back),
    )


def solution(mesh):
    placed = (
        P(("grp", "tp"), None),
        P(("grp", "tp"), None),
        P(("grp", "tp"), None),
        P(("grp", "loc"), None, None),
        P(("grp", "loc"), None, None),
        P(("grp", "loc"), None, "tp"),
    )
    return jax.shard_map(
        body, mesh=mesh, in_specs=placed, out_specs=P(("grp", "tp"), "loc"), check_vma=False
    )
```

```python
import functools

import jax
import jax.numpy as jnp
from jax import lax
from jax.experimental import pallas as pl
from jax.experimental.pallas import tpu as pltpu
from jax.sharding import PartitionSpec as P

VM = pl.BlockSpec(memory_space=pltpu.VMEM)
HBM = pl.BlockSpec(memory_space=pltpu.HBM)
STEP = 256
LANES = 128


def swap_bit(value, axis, bit):
    size = lax.axis_size(axis)
    return lax.ppermute(value, axis, [(i, i ^ bit) for i in range(size)])


def after(value, *others):
    return lax.optimization_barrier((value, others))[0]


def bits_of(size):
    return [1 << i for i in range(size.bit_length() - 1)]


def part_order(size):
    order = [0]
    for bit in reversed(bits_of(size)):
        order = order + [i ^ bit for i in order]
    return order


def call(kernel, outs, arrays, scratch=(), in_specs=None, out_specs=None, flops=None):
    moved = sum(a.size * a.dtype.itemsize for a in (*arrays, *jax.tree.leaves(outs)))
    cost = pl.CostEstimate(flops=flops or 0, bytes_accessed=moved, transcendentals=0)
    return pl.pallas_call(
        kernel,
        out_shape=outs,
        in_specs=in_specs or [VM] * len(arrays),
        out_specs=out_specs or jax.tree.map(lambda _: VM, outs),
        scratch_shapes=list(scratch),
        compiler_params=pltpu.CompilerParams(vmem_limit_bytes=12 << 20),
    )(*arrays)


def rows_at(index, part):
    return pl.ds(pl.multiple_of(index * part, part), part)


def own_expert():
    return lax.axis_index("grp") * lax.axis_size("loc") + lax.axis_index("loc")


def prepare_kernel(part, tokens, ids, weights, message, table, ids_here, weights_here, sems):
    width = tokens.shape[1]
    local = lax.axis_index("loc")
    copies = [
        pltpu.make_async_copy(ids, ids_here, sems.at[0]),
        pltpu.make_async_copy(weights, weights_here, sems.at[1]),
        pltpu.make_async_copy(tokens.at[rows_at(local, part), :], message.at[:, :width], sems.at[2]),
    ]
    for copy in copies:
        copy.start()
    lanes, rows = table.shape[1], table.shape[0]
    expert = lax.broadcasted_iota(jnp.int32, (lanes, rows), 0)
    dense = jnp.zeros((lanes, rows), jnp.float32)
    copies[0].wait()
    copies[1].wait()
    for k in range(ids.shape[0]):
        weight = weights_here[k : k + 1, :].astype(jnp.float32)
        dense = jnp.where(expert == ids_here[k : k + 1, :], weight, dense)
    table[...] = dense.T.astype(jnp.bfloat16)
    message[:, width:] = table[rows_at(local, part), :]
    copies[2].wait()


def hidden_kernel(order, part, *refs):
    *pieces, gate, up, hidden, scale, block, routes, sems = refs
    width = gate.shape[0]
    local = lax.axis_index("loc")
    copies = []
    for n, k in enumerate(order):
        at = slice(n * part, (n + 1) * part)
        if len(pieces) == 2:
            whole = pieces[0].at[rows_at(local ^ k, part), :]
            copies.append(pltpu.make_async_copy(whole, block.at[at, :], sems.at[n]))
            copies[n].start()
            routes[at, :] = pieces[1][rows_at(local ^ k, part), :].astype(jnp.float32)
        else:
            block[at, :] = pieces[n][:, :width]
            routes[at, :] = pieces[n][:, width:].astype(jnp.float32)
    expert = lax.broadcasted_iota(jnp.int32, routes.shape, 1)
    own = jnp.sum(jnp.where(expert == own_expert(), routes[...], 0.0), axis=1, keepdims=True)
    scale[...] = jnp.broadcast_to(own, scale.shape)
    for copy in copies:
        copy.wait()
    for j in range(0, gate.shape[1], STEP):
        a = jnp.dot(block[...], gate[:, j : j + STEP], preferred_element_type=jnp.float32)
        b = jnp.dot(block[...], up[:, j : j + STEP], preferred_element_type=jnp.float32)
        hidden[:, j : j + STEP] = (a / (1.0 + jnp.exp(-a)) * b).astype(jnp.bfloat16)


def column_results(hidden, scale, shards, cols, part_of):
    per_shard = shards[0].shape[1] // cols
    first = (lax.axis_index("loc") % per_shard) ^ part_of
    own = lax.axis_index("tp") ^ (lax.axis_index("loc") // per_shard)
    factor = scale[...]
    for u, weights in enumerate(shards):
        for j in range(0, cols, STEP):
            at = pl.ds(pl.multiple_of(first * cols + j, STEP), STEP)
            out = jnp.dot(hidden[...], weights[:, at], preferred_element_type=jnp.float32)
            out = out.astype(jnp.bfloat16).astype(jnp.float32)
            out = [out[:, i : i + LANES] * factor for i in range(0, STEP, LANES)]
            yield own ^ u, slice(j, j + STEP), jnp.concatenate(out, axis=1)


def leave_kernel(order, part, bit, hidden, scale, *refs):
    *shards, message = refs
    for place, cols, value in column_results(hidden, scale, shards, message.shape[2], bit):
        value = value.astype(jnp.bfloat16)
        for n, k in enumerate(order):
            m = order.index(k ^ bit)
            message[place, n * part : (n + 1) * part, cols] = value[m * part : (m + 1) * part]


def stay_kernel(order, part, bit, with_sum, hidden, scale, *refs):
    if with_sum:
        arrived, *refs = refs
    *shards, keep, message, total = refs
    half = len(shards) // 2
    for place, cols, value in column_results(hidden, scale, shards, total.shape[2], 0):
        if with_sum:
            value = value + arrived[place, :, cols].astype(jnp.float32)
        total[place, :, cols] = value
    for i in range(half):
        keep[i] = total[i]
        for n, k in enumerate(order):
            m = order.index(k ^ bit)
            message[i, n * part : (n + 1) * part, :] = total[half + i, m * part : (m + 1) * part, :].astype(
                jnp.bfloat16
            )


def finish_kernel(order, part, keep, arrived, *refs):
    *others, out = refs
    local = lax.axis_index("loc")
    for n, k in enumerate(order):
        at = slice(n * part, (n + 1) * part)
        value = keep[at, :] + arrived[at, :].astype(jnp.float32)
        for other in others:
            value = value + other[at, :].astype(jnp.float32)
        out[rows_at(local ^ k, part), :] = value.astype(jnp.bfloat16)


def body(tokens, expert_ids, router_weights, w_gate, w_up, w_down):
    groups = lax.axis_size("grp")
    group_size = lax.axis_size("loc")
    tp_size = lax.axis_size("tp")
    rows, width = tokens.shape
    hidden_width = w_gate.shape[2]
    part = rows // group_size
    out_cols = width // group_size
    per_shard = group_size // tp_size
    lanes = -(-groups * group_size // LANES) * LANES
    order = part_order(group_size)
    partners = [1] + list(range(groups - 1, 1, -1))
    shape = jax.ShapeDtypeStruct
    bf16, f32 = jnp.bfloat16, jnp.float32

    message, table = call(
        functools.partial(prepare_kernel, part),
        (shape((part, width + lanes), bf16), shape((rows, lanes), bf16)),
        (tokens, expert_ids.T, router_weights.T),
        in_specs=[HBM] * 3,
        scratch=[
            pltpu.VMEM(expert_ids.shape[::-1], jnp.int32),
            pltpu.VMEM(router_weights.shape[::-1], bf16),
            pltpu.SemaphoreType.DMA((3,)),
        ],
    )

    down = [w_down[0]]
    for bit in bits_of(tp_size):
        down = down + [swap_bit(value, "tp", bit) for value in down]

    def ffn(pieces):
        return call(
            functools.partial(hidden_kernel, order, part),
            (shape((rows, hidden_width), bf16), shape((rows, LANES), f32)),
            (*pieces, w_gate[0], w_up[0]),
            in_specs=[HBM] + [VM] * 3 if len(pieces) == 2 else None,
            scratch=[
                pltpu.VMEM((rows, width), bf16),
                pltpu.VMEM((rows, lanes), f32),
                pltpu.SemaphoreType.DMA((len(order),)),
            ],
            flops=4 * rows * width * hidden_width,
        )

    flops = 2 * rows * hidden_width * out_cols * tp_size

    def leave(hidden, scale):
        message = call(
            functools.partial(leave_kernel, order, part, 1),
            shape((tp_size, rows, out_cols), bf16),
            (hidden, scale, *down),
            flops=flops,
        )
        return swap_bit(message, "loc", 1)

    def stay(hidden, scale, arrived):
        half = tp_size // 2
        return call(
            functools.partial(stay_kernel, order, part, half * per_shard, len(arrived) > 0),
            (shape((half, rows, out_cols), f32), shape((half, rows, out_cols), bf16)),
            (hidden, scale, *arrived, *down),
            scratch=[pltpu.VMEM((tp_size, rows, out_cols), f32)],
            flops=flops,
        )

    def across(keep, message):
        half = tp_size // 2
        arrived = swap_bit(message, "loc", half * per_shard)
        while half > 1:
            half = half // 2
            keep = keep + arrived.astype(f32)
            bit = half * per_shard
            there = [order.index(k ^ bit) for k in order]
            message = keep[half:].astype(bf16).reshape(half, group_size, part, out_cols)
            message = jnp.stack([message[:, m] for m in there], axis=1)
            arrived = swap_bit(message.reshape(half, rows, out_cols), "loc", bit)
            keep = keep[:half]
        return keep[0], arrived[0]

    sent, hidden = {}, {0: ffn([tokens, table])}
    for s in partners:
        sent[s] = swap_bit(message, "grp", s)
    for n, s in enumerate(partners):
        pieces = [after(sent[s], hidden[0])]
        for bit in reversed(bits_of(group_size)):
            if n > 0 and bit == 1:
                pieces[1:] = [after(value, hidden[partners[n - 1]]) for value in pieces[1:]]
            pieces = pieces + [swap_bit(value, "loc", bit) for value in pieces]
        hidden[s] = ffn(pieces)

    turns = partners[1:2] + partners[:1] + partners[2:] + [0]
    left, stayed, sums, back = {}, {}, {}, {}

    def first_half(n):
        if n < len(turns):
            s = turns[n]
            order_after = [stayed[turns[n - 2]]] if n > 1 else [left[turns[n - 1]]] if n > 0 else []
            left[s] = [leave(*after(hidden[s], *order_after))] if per_shard == 2 else []

    first_half(0)
    first_half(1)
    for n, s in enumerate(turns):
        order_after = [stayed[turns[n - 1]]] if n > 0 else []
        stayed[s] = stay(*after(hidden[s], *order_after), left[s])
        first_half(n + 2)
    for n, s in enumerate(turns):
        keep, message = stayed[s]
        if n > 1:
            message = after(message, sums[turns[n - 2]][1])
        keep, arrived = across(keep, message)
        sums[s] = keep, arrived
        if s > 0:
            both = (keep + arrived.astype(f32)).astype(bf16)
            back[s] = swap_bit(both, "grp", s)
    return call(
        functools.partial(finish_kernel, order, part),
        shape((rows, out_cols), bf16),
        (*sums[0], *back.values()),
    )


def solution(mesh):
    placed = (
        P(("grp", "tp"), None),
        P(("grp", "tp"), None),
        P(("grp", "tp"), None),
        P(("grp", "loc"), None, None),
        P(("grp", "loc"), None, None),
        P(("grp", "loc"), None, "tp"),
    )
    return jax.shard_map(
        body, mesh=mesh, in_specs=placed, out_specs=P(("grp", "tp"), "loc"), check_vma=False
    )
```

```python
import functools

import jax
import jax.numpy as jnp
from jax import lax
from jax.experimental import pallas as pl
from jax.experimental.pallas import tpu as pltpu
from jax.sharding import PartitionSpec as P

VM = pl.BlockSpec(memory_space=pltpu.VMEM)
HBM = pl.BlockSpec(memory_space=pltpu.HBM)
STEP = 256
LANES = 128


def swap_bit(value, axis, bit):
    size = lax.axis_size(axis)
    return lax.ppermute(value, axis, [(i, i ^ bit) for i in range(size)])


def after(value, *others):
    return lax.optimization_barrier((value, others))[0]


def bits_of(size):
    return [1 << i for i in range(size.bit_length() - 1)]


def part_order(size):
    order = [0]
    for bit in reversed(bits_of(size)):
        order = order + [i ^ bit for i in order]
    return order


def call(kernel, outs, arrays, scratch=(), in_specs=None, out_specs=None, flops=None):
    moved = sum(a.size * a.dtype.itemsize for a in (*arrays, *jax.tree.leaves(outs)))
    cost = pl.CostEstimate(flops=flops or 0, bytes_accessed=moved, transcendentals=0)
    return pl.pallas_call(
        kernel,
        out_shape=outs,
        in_specs=in_specs or [VM] * len(arrays),
        out_specs=out_specs or jax.tree.map(lambda _: VM, outs),
        scratch_shapes=list(scratch),
        cost_estimate=cost if flops else None,
        compiler_params=pltpu.CompilerParams(vmem_limit_bytes=12 << 20),
    )(*arrays)


def rows_at(index, part):
    return pl.ds(pl.multiple_of(index * part, part), part)


def own_expert():
    return lax.axis_index("grp") * lax.axis_size("loc") + lax.axis_index("loc")


def prepare_kernel(part, tokens, routes, message, table, routes_here, sems):
    width = tokens.shape[1]
    local = lax.axis_index("loc")
    copies = [
        pltpu.make_async_copy(routes, routes_here, sems.at[0]),
        pltpu.make_async_copy(tokens.at[rows_at(local, part), :], message.at[:, :width], sems.at[1]),
    ]
    for copy in copies:
        copy.start()
    lanes, rows = table.shape[1], table.shape[0]
    expert = lax.broadcasted_iota(jnp.int32, (lanes, rows), 0).astype(jnp.float32)
    dense = jnp.zeros((lanes, rows), jnp.float32)
    copies[0].wait()
    choices = routes.shape[0] // 2
    for k in range(choices):
        weight = routes_here[choices + k : choices + k + 1, :]
        dense = jnp.where(expert == routes_here[k : k + 1, :], weight, dense)
    table[...] = dense.T.astype(jnp.bfloat16)
    message[:, width:] = table[rows_at(local, part), :]
    copies[1].wait()


def hidden_kernel(order, part, own, *refs):
    *pieces, gate, up, hidden, scale, block, routes, sems = refs
    width = gate.shape[0]
    local = lax.axis_index("loc")
    copies = []
    for n, k in enumerate(order):
        at = slice(n * part, (n + 1) * part)
        if own:
            whole = pieces[0].at[rows_at(local ^ k, part), :]
            copies.append(pltpu.make_async_copy(whole, block.at[at, :], sems.at[n]))
            copies[n].start()
            routes[at, :] = pieces[1][rows_at(local ^ k, part), :].astype(jnp.float32)
        else:
            block[at, :] = pieces[n][:, :width]
            routes[at, :] = pieces[n][:, width:].astype(jnp.float32)
    expert = lax.broadcasted_iota(jnp.int32, routes.shape, 1)
    own = jnp.sum(jnp.where(expert == own_expert(), routes[...], 0.0), axis=1, keepdims=True)
    scale[...] = jnp.broadcast_to(own, scale.shape)
    for copy in copies:
        copy.wait()
    for j in range(0, gate.shape[1], STEP):
        a = jnp.dot(block[...], gate[:, j : j + STEP], preferred_element_type=jnp.float32)
        b = jnp.dot(block[...], up[:, j : j + STEP], preferred_element_type=jnp.float32)
        hidden[:, j : j + STEP] = (a / (1.0 + jnp.exp(-a)) * b).astype(jnp.bfloat16)


def column_results(hidden, scale, shards, cols, part_of):
    per_shard = shards[0].shape[1] // cols
    first = (lax.axis_index("loc") % per_shard) ^ part_of
    own = lax.axis_index("tp") ^ (lax.axis_index("loc") // per_shard)
    factor = scale[...]
    for u, weights in enumerate(shards):
        for j in range(0, cols, STEP):
            at = pl.ds(pl.multiple_of(first * cols + j, STEP), STEP)
            out = jnp.dot(hidden[...], weights[:, at], preferred_element_type=jnp.float32)
            out = out.astype(jnp.bfloat16).astype(jnp.float32)
            out = [out[:, i : i + LANES] * factor for i in range(0, STEP, LANES)]
            yield own ^ u, slice(j, j + STEP), jnp.concatenate(out, axis=1)


def leave_kernel(order, part, bit, hidden, scale, *refs):
    *shards, message = refs
    for place, cols, value in column_results(hidden, scale, shards, message.shape[2], bit):
        value = value.astype(jnp.bfloat16)
        for n, k in enumerate(order):
            m = order.index(k ^ bit)
            message[place, n * part : (n + 1) * part, cols] = value[m * part : (m + 1) * part]


def stay_kernel(order, part, bit, with_sum, hidden, scale, *refs):
    arrived, refs = refs[:with_sum], refs[with_sum:]
    *shards, keep, message, total = refs
    half = len(shards) // 2
    for place, cols, value in column_results(hidden, scale, shards, total.shape[2], 0):
        if with_sum:
            value = value + jnp.concatenate([a[place, :, cols] for a in arrived], axis=0).astype(jnp.float32)
        total[place, :, cols] = value
    for i in range(half):
        keep[i] = total[i]
        for n, k in enumerate(order):
            m = order.index(k ^ bit)
            message[i, n * part : (n + 1) * part, :] = total[half + i, m * part : (m + 1) * part, :].astype(
                jnp.bfloat16
            )


def finish_kernel(order, part, keep, arrived, *refs):
    *others, out = refs
    local = lax.axis_index("loc")
    for n, k in enumerate(order):
        at = slice(n * part, (n + 1) * part)
        value = keep[at, :] + arrived[at, :].astype(jnp.float32)
        for other in others:
            value = value + other[at, :].astype(jnp.float32)
        out[rows_at(local ^ k, part), :] = value.astype(jnp.bfloat16)


def body(tokens, expert_ids, router_weights, w_gate, w_up, w_down):
    groups = lax.axis_size("grp")
    group_size = lax.axis_size("loc")
    tp_size = lax.axis_size("tp")
    rows, width = tokens.shape
    hidden_width = w_gate.shape[2]
    part = rows // group_size
    out_cols = width // group_size
    per_shard = group_size // tp_size
    lanes = -(-groups * group_size // LANES) * LANES
    order = part_order(group_size)
    partners = [1] + list(range(groups - 1, 1, -1))
    shape = jax.ShapeDtypeStruct
    bf16, f32 = jnp.bfloat16, jnp.float32

    routes = jnp.concatenate([expert_ids.T.astype(f32), router_weights.T.astype(f32)], axis=0)
    message, table = call(
        functools.partial(prepare_kernel, part),
        (shape((part, width + lanes), bf16), shape((rows, lanes), bf16)),
        (tokens, routes),
        in_specs=[HBM] * 2,
        scratch=[pltpu.VMEM(routes.shape, f32), pltpu.SemaphoreType.DMA((2,))],
    )

    down = [w_down[0]]
    for bit in bits_of(tp_size):
        down = down + [swap_bit(value, "tp", bit) for value in down]

    def ffn(pieces, own=False):
        return call(
            functools.partial(hidden_kernel, order, part, own),
            (shape((rows, hidden_width), bf16), shape((rows, LANES), f32)),
            (*pieces, w_gate[0], w_up[0]),
            in_specs=[HBM] + [VM] * 3 if own else None,
            scratch=[
                pltpu.VMEM((rows, width), bf16),
                pltpu.VMEM((rows, lanes), f32),
                pltpu.SemaphoreType.DMA((len(order),)),
            ],
            flops=4 * rows * width * hidden_width,
        )

    flops = 2 * rows * hidden_width * out_cols * tp_size

    def leave(hidden, scale):
        message = call(
            functools.partial(leave_kernel, order, part, 1),
            shape((tp_size, rows, out_cols), bf16),
            (hidden, scale, *down),
            flops=flops,
        )
        return swap_bit(message, "loc", 1)

    def stay(hidden, scale, arrived):
        half = tp_size // 2
        return call(
            functools.partial(stay_kernel, order, part, half * per_shard, len(arrived)),
            (shape((half, rows, out_cols), f32), shape((half, rows, out_cols), bf16)),
            (hidden, scale, *arrived, *down),
            scratch=[pltpu.VMEM((tp_size, rows, out_cols), f32)],
            flops=flops,
        )

    def across(keep, message):
        half = tp_size // 2
        arrived = swap_bit(message, "loc", half * per_shard)
        while half > 1:
            half = half // 2
            keep = keep + arrived.astype(f32)
            bit = half * per_shard
            there = [order.index(k ^ bit) for k in order]
            message = keep[half:].astype(bf16).reshape(half, group_size, part, out_cols)
            message = jnp.stack([message[:, m] for m in there], axis=1)
            arrived = swap_bit(message.reshape(half, rows, out_cols), "loc", bit)
            keep = keep[:half]
        return keep[0], arrived

    sent = {s: swap_bit(message, "grp", s) for s in partners}
    turns = partners[1:] + partners[:1] + [0]
    first, late = turns[0], partners[-1]
    hidden, left, stayed, sums, back = {}, {}, {}, {}, {}

    def first_half(s):
        if s not in left:
            left[s] = [leave(*hidden[s])] if per_shard == 2 else []

    hidden[0] = ffn([tokens, table], own=True)
    for s in partners:
        pieces = [after(sent[s], hidden[0])]
        for bit in reversed(bits_of(group_size)):
            if bit == 1 and s == late:
                ready = [hidden[other] for other in partners[:-1]]
                pieces[1:] = [after(value, ready) for value in pieces[1:]]
            pieces = pieces + [swap_bit(value, "loc", bit) for value in pieces]
        if s == late:
            first_half(first)
            pieces = after(pieces, left[first])
        hidden[s] = ffn(pieces)

    for n, s in enumerate(turns):
        for other in turns[n : n + 2]:
            first_half(other)
        stayed[s] = stay(*hidden[s], left[s])
    for n, s in enumerate(turns):
        keep, message = stayed[s]
        if n > 0:
            message = after(message, sums[turns[max(n - 2, 0)]][1])
        sums[s] = keep, arrived = across(keep, message)
        if s > 0:
            both = (keep + arrived[0].astype(f32)).astype(bf16)
            back[s] = swap_bit(both, "grp", s)
    return call(
        functools.partial(finish_kernel, order, part),
        shape((rows, out_cols), bf16),
        (sums[0][0], sums[0][1][0], *back.values()),
    )


def solution(mesh):
    placed = (
        P(("grp", "tp"), None),
        P(("grp", "tp"), None),
        P(("grp", "tp"), None),
        P(("grp", "loc"), None, None),
        P(("grp", "loc"), None, None),
        P(("grp", "loc"), None, "tp"),
    )
    return jax.shard_map(
        body, mesh=mesh, in_specs=placed, out_specs=P(("grp", "tp"), "loc"), check_vma=False
    )
```

```python
import functools

import jax
import jax.numpy as jnp
from jax import lax
from jax.experimental import pallas as pl
from jax.experimental.pallas import tpu as pltpu
from jax.sharding import PartitionSpec as P

VM = pl.BlockSpec(memory_space=pltpu.VMEM)
HBM = pl.BlockSpec(memory_space=pltpu.HBM)
STEP = 256
LANES = 128


def swap_bit(value, axis, bit):
    size = lax.axis_size(axis)
    return lax.ppermute(value, axis, [(i, i ^ bit) for i in range(size)])


def after(value, *others):
    return lax.optimization_barrier((value, others))[0]


def bits_of(size):
    return [1 << i for i in range(size.bit_length() - 1)]


def part_order(size):
    order = [0]
    for bit in reversed(bits_of(size)):
        order = order + [i ^ bit for i in order]
    return order


def call(kernel, outs, arrays, scratch=(), in_specs=None, out_specs=None, flops=None):
    moved = sum(a.size * a.dtype.itemsize for a in (*arrays, *jax.tree.leaves(outs)))
    cost = pl.CostEstimate(flops=flops or 0, bytes_accessed=moved, transcendentals=0)
    return pl.pallas_call(
        kernel,
        out_shape=outs,
        in_specs=in_specs or [VM] * len(arrays),
        out_specs=out_specs or jax.tree.map(lambda _: VM, outs),
        scratch_shapes=list(scratch),
        cost_estimate=cost if flops else None,
        compiler_params=pltpu.CompilerParams(vmem_limit_bytes=12 << 20),
    )(*arrays)


def rows_at(index, part):
    return pl.ds(pl.multiple_of(index * part, part), part)


def own_expert():
    return lax.axis_index("grp") * lax.axis_size("loc") + lax.axis_index("loc")


def prepare_kernel(part, tokens, routes, message, table, routes_here, sems):
    width = tokens.shape[1]
    local = lax.axis_index("loc")
    copies = [
        pltpu.make_async_copy(routes, routes_here, sems.at[0]),
        pltpu.make_async_copy(tokens.at[rows_at(local, part), :], message.at[:, :width], sems.at[1]),
    ]
    for copy in copies:
        copy.start()
    lanes, rows = table.shape[1], table.shape[0]
    expert = lax.broadcasted_iota(jnp.int32, (lanes, rows), 0).astype(jnp.float32)
    dense = jnp.zeros((lanes, rows), jnp.float32)
    copies[0].wait()
    choices = routes.shape[0] // 2
    for k in range(choices):
        weight = routes_here[choices + k : choices + k + 1, :]
        dense = jnp.where(expert == routes_here[k : k + 1, :], weight, dense)
    table[...] = dense.T.astype(jnp.bfloat16)
    message[:, width:] = table[rows_at(local, part), :]
    copies[1].wait()


def hidden_kernel(order, part, own, *refs):
    *pieces, gate, up, hidden, scale, block, routes, sems = refs
    width = gate.shape[0]
    local = lax.axis_index("loc")
    copies = []
    for n, k in enumerate(order):
        at = slice(n * part, (n + 1) * part)
        if own:
            whole = pieces[0].at[rows_at(local ^ k, part), :]
            copies.append(pltpu.make_async_copy(whole, block.at[at, :], sems.at[n]))
            copies[n].start()
            routes[at, :] = pieces[1][rows_at(local ^ k, part), :].astype(jnp.float32)
        else:
            block[at, :] = pieces[n][:, :width]
            routes[at, :] = pieces[n][:, width:].astype(jnp.float32)
    expert = lax.broadcasted_iota(jnp.int32, routes.shape, 1)
    own = jnp.sum(jnp.where(expert == own_expert(), routes[...], 0.0), axis=1, keepdims=True)
    scale[...] = jnp.broadcast_to(own, scale.shape)
    for copy in copies:
        copy.wait()
    for j in range(0, gate.shape[1], STEP):
        a = jnp.dot(block[...], gate[:, j : j + STEP], preferred_element_type=jnp.float32)
        b = jnp.dot(block[...], up[:, j : j + STEP], preferred_element_type=jnp.float32)
        hidden[:, j : j + STEP] = (a / (1.0 + jnp.exp(-a)) * b).astype(jnp.bfloat16)


def column_results(hidden, scale, shards, cols, part_of):
    per_shard = shards[0].shape[1] // cols
    first = (lax.axis_index("loc") % per_shard) ^ part_of
    own = lax.axis_index("tp") ^ (lax.axis_index("loc") // per_shard)
    factor = scale[...]
    for u, weights in enumerate(shards):
        for j in range(0, cols, STEP):
            at = pl.ds(pl.multiple_of(first * cols + j, STEP), STEP)
            out = jnp.dot(hidden[...], weights[:, at], preferred_element_type=jnp.float32)
            out = out.astype(jnp.bfloat16).astype(jnp.float32)
            out = [out[:, i : i + LANES] * factor for i in range(0, STEP, LANES)]
            yield own ^ u, slice(j, j + STEP), jnp.concatenate(out, axis=1)


def leave_kernel(order, part, bit, hidden, scale, *refs):
    *shards, message = refs
    for place, cols, value in column_results(hidden, scale, shards, message.shape[2], bit):
        value = value.astype(jnp.bfloat16)
        for n, k in enumerate(order):
            m = order.index(k ^ bit)
            message[place, n * part : (n + 1) * part, cols] = value[m * part : (m + 1) * part]


def stay_kernel(order, part, bit, with_sum, hidden, scale, *refs):
    arrived, refs = refs[:with_sum], refs[with_sum:]
    *shards, keep, message, total = refs
    half = len(shards) // 2
    for place, cols, value in column_results(hidden, scale, shards, total.shape[2], 0):
        if with_sum:
            value = value + jnp.concatenate([a[place, :, cols] for a in arrived], axis=0).astype(jnp.float32)
        total[place, :, cols] = value
    for i in range(half):
        keep[i] = total[i]
        for n, k in enumerate(order):
            m = order.index(k ^ bit)
            message[i, n * part : (n + 1) * part, :] = total[half + i, m * part : (m + 1) * part, :].astype(
                jnp.bfloat16
            )


def finish_kernel(order, part, keep, arrived, *refs):
    *others, out = refs
    local = lax.axis_index("loc")
    for n, k in enumerate(order):
        at = slice(n * part, (n + 1) * part)
        value = keep[at, :] + arrived[at, :].astype(jnp.float32)
        for other in others:
            value = value + other[at, :].astype(jnp.float32)
        out[rows_at(local ^ k, part), :] = value.astype(jnp.bfloat16)


def body(tokens, expert_ids, router_weights, w_gate, w_up, w_down):
    groups = lax.axis_size("grp")
    group_size = lax.axis_size("loc")
    tp_size = lax.axis_size("tp")
    rows, width = tokens.shape
    hidden_width = w_gate.shape[2]
    part = rows // group_size
    out_cols = width // group_size
    per_shard = group_size // tp_size
    lanes = -(-groups * group_size // LANES) * LANES
    order = part_order(group_size)
    partners = list(range(1, groups))
    shape = jax.ShapeDtypeStruct
    bf16, f32 = jnp.bfloat16, jnp.float32

    routes = jnp.concatenate([expert_ids.T.astype(f32), router_weights.T.astype(f32)], axis=0)
    message, table = call(
        functools.partial(prepare_kernel, part),
        (shape((part, width + lanes), bf16), shape((rows, lanes), bf16)),
        (tokens, routes),
        in_specs=[HBM] * 2,
        scratch=[pltpu.VMEM(routes.shape, f32), pltpu.SemaphoreType.DMA((2,))],
    )

    down = [w_down[0]]
    for bit in bits_of(tp_size):
        down = down + [swap_bit(value, "tp", bit) for value in down]

    def ffn(pieces, own=False):
        return call(
            functools.partial(hidden_kernel, order, part, own),
            (shape((rows, hidden_width), bf16), shape((rows, LANES), f32)),
            (*pieces, w_gate[0], w_up[0]),
            in_specs=[HBM] + [VM] * 3 if own else None,
            scratch=[
                pltpu.VMEM((rows, width), bf16),
                pltpu.VMEM((rows, lanes), f32),
                pltpu.SemaphoreType.DMA((len(order),)),
            ],
            flops=4 * rows * width * hidden_width,
        )

    flops = 2 * rows * hidden_width * out_cols * tp_size

    def leave(hidden, scale):
        message = call(
            functools.partial(leave_kernel, order, part, 1),
            shape((tp_size, rows, out_cols), bf16),
            (hidden, scale, *down),
            flops=flops,
        )
        return swap_bit(message, "loc", 1)

    def stay(hidden, scale, arrived):
        half = tp_size // 2
        return call(
            functools.partial(stay_kernel, order, part, half * per_shard, len(arrived)),
            (shape((half, rows, out_cols), f32), shape((half, rows, out_cols), bf16)),
            (hidden, scale, *arrived, *down),
            scratch=[pltpu.VMEM((tp_size, rows, out_cols), f32)],
            flops=flops,
        )

    def across(keep, message):
        half = tp_size // 2
        arrived = swap_bit(message, "loc", half * per_shard)
        while half > 1:
            half = half // 2
            keep = keep + arrived.astype(f32)
            bit = half * per_shard
            there = [order.index(k ^ bit) for k in order]
            message = keep[half:].astype(bf16).reshape(half, group_size, part, out_cols)
            message = jnp.stack([message[:, m] for m in there], axis=1)
            arrived = swap_bit(message.reshape(half, rows, out_cols), "loc", bit)
            keep = keep[:half]
        return keep[0], arrived

    sent = {s: swap_bit(message, "grp", s) for s in partners}
    turns = partners[1:] + partners[:1] + [0]
    first, late = turns[0], partners[-1]
    hidden, left, stayed, sums, back = {}, {}, {}, {}, {}

    def first_half(s):
        if s not in left:
            left[s] = [leave(*hidden[s])] if per_shard == 2 else []

    hidden[0] = ffn([tokens, table], own=True)
    for s in partners:
        pieces = [after(sent[s], hidden[0])]
        for bit in reversed(bits_of(group_size)):
            if bit == 1 and s == late:
                ready = [hidden[other] for other in partners[:-1]]
                pieces[1:] = [after(value, ready) for value in pieces[1:]]
            pieces = pieces + [swap_bit(value, "loc", bit) for value in pieces]
        if s == late:
            first_half(first)
            pieces = after(pieces, left[first])
        hidden[s] = ffn(pieces)

    for n, s in enumerate(turns):
        for other in turns[n : n + 2]:
            first_half(other)
        stayed[s] = stay(*hidden[s], left[s])
    for n, s in enumerate(turns):
        keep, message = stayed[s]
        if n > 0:
            message = after(message, sums[turns[max(n - 2, 0)]][1])
        sums[s] = keep, arrived = across(keep, message)
        if s > 0:
            both = (keep + arrived[0].astype(f32)).astype(bf16)
            back[s] = swap_bit(both, "grp", s)
    return call(
        functools.partial(finish_kernel, order, part),
        shape((rows, out_cols), bf16),
        (sums[0][0], sums[0][1][0], *back.values()),
    )


def solution(mesh):
    placed = (
        P(("grp", "tp"), None),
        P(("grp", "tp"), None),
        P(("grp", "tp"), None),
        P(("grp", "loc"), None, None),
        P(("grp", "loc"), None, None),
        P(("grp", "loc"), None, "tp"),
    )
    return jax.shard_map(
        body, mesh=mesh, in_specs=placed, out_specs=P(("grp", "tp"), "loc"), check_vma=False
    )
```

```python
import functools

import jax
import jax.numpy as jnp
from jax import lax
from jax.experimental import pallas as pl
from jax.experimental.pallas import tpu as pltpu
from jax.sharding import PartitionSpec as P

VM = pl.BlockSpec(memory_space=pltpu.VMEM)
HBM = pl.BlockSpec(memory_space=pltpu.HBM)
STEP = 256
LANES = 128


def swap_bit(value, axis, bit):
    size = lax.axis_size(axis)
    return lax.ppermute(value, axis, [(i, i ^ bit) for i in range(size)])


def after(value, *others):
    return lax.optimization_barrier((value, others))[0]


def bits_of(size):
    return [1 << i for i in range(size.bit_length() - 1)]


def part_order(size):
    order = [0]
    for bit in reversed(bits_of(size)):
        order = order + [i ^ bit for i in order]
    return order


def call(kernel, outs, arrays, scratch=(), in_specs=None, out_specs=None, flops=None):
    moved = sum(a.size * a.dtype.itemsize for a in (*arrays, *jax.tree.leaves(outs)))
    cost = pl.CostEstimate(flops=flops or 0, bytes_accessed=moved, transcendentals=0)
    return pl.pallas_call(
        kernel,
        out_shape=outs,
        in_specs=in_specs or [VM] * len(arrays),
        out_specs=out_specs or jax.tree.map(lambda _: VM, outs),
        scratch_shapes=list(scratch),
        cost_estimate=cost if flops else None,
        compiler_params=pltpu.CompilerParams(vmem_limit_bytes=12 << 20),
    )(*arrays)


def rows_at(index, part):
    return pl.ds(pl.multiple_of(index * part, part), part)


def own_expert():
    return lax.axis_index("grp") * lax.axis_size("loc") + lax.axis_index("loc")


def prepare_kernel(part, tokens, routes, message, table, routes_here, sems):
    width = tokens.shape[1]
    local = lax.axis_index("loc")
    copies = [
        pltpu.make_async_copy(routes, routes_here, sems.at[0]),
        pltpu.make_async_copy(tokens.at[rows_at(local, part), :], message.at[:, :width], sems.at[1]),
    ]
    for copy in copies:
        copy.start()
    lanes, rows = table.shape[1], table.shape[0]
    expert = lax.broadcasted_iota(jnp.int32, (lanes, rows), 0).astype(jnp.float32)
    dense = jnp.zeros((lanes, rows), jnp.float32)
    copies[0].wait()
    choices = routes.shape[0] // 2
    for k in range(choices):
        weight = routes_here[choices + k : choices + k + 1, :]
        dense = jnp.where(expert == routes_here[k : k + 1, :], weight, dense)
    table[...] = dense.T.astype(jnp.bfloat16)
    message[:, width:] = table[rows_at(local, part), :]
    copies[1].wait()


def hidden_kernel(order, part, own, *refs):
    *pieces, gate, up, hidden, scale, block, routes, sems = refs
    width = gate.shape[0]
    local = lax.axis_index("loc")
    copies = []
    for n, k in enumerate(order):
        at = slice(n * part, (n + 1) * part)
        if own:
            whole = pieces[0].at[rows_at(local ^ k, part), :]
            copies.append(pltpu.make_async_copy(whole, block.at[at, :], sems.at[n]))
            copies[n].start()
            routes[at, :] = pieces[1][rows_at(local ^ k, part), :].astype(jnp.float32)
        else:
            block[at, :] = pieces[n][:, :width]
            routes[at, :] = pieces[n][:, width:].astype(jnp.float32)
    expert = lax.broadcasted_iota(jnp.int32, routes.shape, 1)
    own = jnp.sum(jnp.where(expert == own_expert(), routes[...], 0.0), axis=1, keepdims=True)
    scale[...] = jnp.broadcast_to(own, scale.shape)
    for copy in copies:
        copy.wait()
    for j in range(0, gate.shape[1], STEP):
        a = jnp.dot(block[...], gate[:, j : j + STEP], preferred_element_type=jnp.float32)
        b = jnp.dot(block[...], up[:, j : j + STEP], preferred_element_type=jnp.float32)
        hidden[:, j : j + STEP] = (a / (1.0 + jnp.exp(-a)) * b).astype(jnp.bfloat16)


def column_results(hidden, scale, shards, cols, part_of):
    per_shard = shards[0].shape[1] // cols
    first = (lax.axis_index("loc") % per_shard) ^ part_of
    own = lax.axis_index("tp") ^ (lax.axis_index("loc") // per_shard)
    factor = scale[...]
    for u, weights in enumerate(shards):
        for j in range(0, cols, STEP):
            at = pl.ds(pl.multiple_of(first * cols + j, STEP), STEP)
            out = jnp.dot(hidden[...], weights[:, at], preferred_element_type=jnp.float32)
            out = out.astype(jnp.bfloat16).astype(jnp.float32)
            out = [out[:, i : i + LANES] * factor for i in range(0, STEP, LANES)]
            yield own ^ u, slice(j, j + STEP), jnp.concatenate(out, axis=1)


def leave_kernel(order, part, bit, hidden, scale, *refs):
    *shards, message = refs
    for place, cols, value in column_results(hidden, scale, shards, message.shape[2], bit):
        value = value.astype(jnp.bfloat16)
        for n, k in enumerate(order):
            m = order.index(k ^ bit)
            message[place, n * part : (n + 1) * part, cols] = value[m * part : (m + 1) * part]


def stay_kernel(order, part, bit, with_sum, hidden, scale, *refs):
    arrived, refs = refs[:with_sum], refs[with_sum:]
    *shards, keep, message, total = refs
    half = len(shards) // 2
    for place, cols, value in column_results(hidden, scale, shards, total.shape[2], 0):
        if with_sum:
            value = value + jnp.concatenate([a[place, :, cols] for a in arrived], axis=0).astype(jnp.float32)
        total[place, :, cols] = value
    for i in range(half):
        keep[i] = total[i]
        for n, k in enumerate(order):
            m = order.index(k ^ bit)
            message[i, n * part : (n + 1) * part, :] = total[half + i, m * part : (m + 1) * part, :].astype(
                jnp.bfloat16
            )


def finish_kernel(order, part, keep, arrived, *refs):
    *others, out = refs
    local = lax.axis_index("loc")
    for n, k in enumerate(order):
        at = slice(n * part, (n + 1) * part)
        value = keep[at, :] + arrived[at, :].astype(jnp.float32)
        for other in others:
            value = value + other[at, :].astype(jnp.float32)
        out[rows_at(local ^ k, part), :] = value.astype(jnp.bfloat16)


def body(tokens, expert_ids, router_weights, w_gate, w_up, w_down):
    groups = lax.axis_size("grp")
    group_size = lax.axis_size("loc")
    tp_size = lax.axis_size("tp")
    rows, width = tokens.shape
    hidden_width = w_gate.shape[2]
    part = rows // group_size
    out_cols = width // group_size
    per_shard = group_size // tp_size
    lanes = -(-groups * group_size // LANES) * LANES
    order = part_order(group_size)
    partners = list(range(1, groups))
    shape = jax.ShapeDtypeStruct
    bf16, f32 = jnp.bfloat16, jnp.float32

    routes = jnp.concatenate([expert_ids.T.astype(f32), router_weights.T.astype(f32)], axis=0)
    message, table = call(
        functools.partial(prepare_kernel, part),
        (shape((part, width + lanes), bf16), shape((rows, lanes), bf16)),
        (tokens, routes),
        in_specs=[HBM] * 2,
        scratch=[pltpu.VMEM(routes.shape, f32), pltpu.SemaphoreType.DMA((2,))],
    )

    down = [w_down[0]]
    for bit in bits_of(tp_size):
        down = down + [swap_bit(value, "tp", bit) for value in down]

    def ffn(pieces, own=False):
        return call(
            functools.partial(hidden_kernel, order, part, own),
            (shape((rows, hidden_width), bf16), shape((rows, LANES), f32)),
            (*pieces, w_gate[0], w_up[0]),
            in_specs=[HBM] + [VM] * 3 if own else None,
            scratch=[
                pltpu.VMEM((rows, width), bf16),
                pltpu.VMEM((rows, lanes), f32),
                pltpu.SemaphoreType.DMA((len(order),)),
            ],
            flops=4 * rows * width * hidden_width,
        )

    flops = 2 * rows * hidden_width * out_cols * tp_size

    def leave(hidden, scale):
        message = call(
            functools.partial(leave_kernel, order, part, 1),
            shape((tp_size, rows, out_cols), bf16),
            (hidden, scale, *down),
            flops=flops,
        )
        return swap_bit(message, "loc", 1)

    def stay(hidden, scale, arrived):
        half = tp_size // 2
        return call(
            functools.partial(stay_kernel, order, part, half * per_shard, len(arrived)),
            (shape((half, rows, out_cols), f32), shape((half, rows, out_cols), bf16)),
            (hidden, scale, *arrived, *down),
            scratch=[pltpu.VMEM((tp_size, rows, out_cols), f32)],
            flops=flops,
        )

    def across(keep, message):
        half = tp_size // 2
        arrived = swap_bit(message, "loc", half * per_shard)
        while half > 1:
            half = half // 2
            keep = keep + arrived.astype(f32)
            bit = half * per_shard
            there = [order.index(k ^ bit) for k in order]
            message = keep[half:].astype(bf16).reshape(half, group_size, part, out_cols)
            message = jnp.stack([message[:, m] for m in there], axis=1)
            arrived = swap_bit(message.reshape(half, rows, out_cols), "loc", bit)
            keep = keep[:half]
        return keep[0], arrived

    sent = {s: swap_bit(message, "grp", s) for s in partners}
    turns = partners[1:] + partners[:1] + [0]
    first, late = turns[0], partners[-1]
    hidden, left, stayed, sums, back = {}, {}, {}, {}, {}

    def first_half(s):
        if s not in left:
            left[s] = [leave(*hidden[s])] if per_shard == 2 else []

    hidden[0] = ffn([tokens, table], own=True)
    for s in partners:
        pieces = [after(sent[s], hidden[0])]
        for bit in reversed(bits_of(group_size)):
            if bit == 1 and s == late:
                ready = [hidden[other] for other in partners[:-1]]
                pieces[1:] = [after(value, ready) for value in pieces[1:]]
            pieces = pieces + [swap_bit(value, "loc", bit) for value in pieces]
        if s == late:
            first_half(first)
            pieces = after(pieces, left[first])
        hidden[s] = ffn(pieces)

    for n, s in enumerate(turns):
        for other in turns[n : n + 2]:
            first_half(other)
        stayed[s] = stay(*hidden[s], left[s])
    for n, s in enumerate(turns):
        keep, message = stayed[s]
        if n > 1:
            message = after(message, sums[turns[max(n - 2, 0)]][1])
        sums[s] = keep, arrived = across(keep, message)
        if s > 0:
            both = (keep + arrived[0].astype(f32)).astype(bf16)
            back[s] = swap_bit(both, "grp", s)
    return call(
        functools.partial(finish_kernel, order, part),
        shape((rows, out_cols), bf16),
        (sums[0][0], sums[0][1][0], *back.values()),
    )


def solution(mesh):
    placed = (
        P(("grp", "tp"), None),
        P(("grp", "tp"), None),
        P(("grp", "tp"), None),
        P(("grp", "loc"), None, None),
        P(("grp", "loc"), None, None),
        P(("grp", "loc"), None, "tp"),
    )
    return jax.shard_map(
        body, mesh=mesh, in_specs=placed, out_specs=P(("grp", "tp"), "loc"), check_vma=False
    )
```
